32 devices in a mesh: tok: 8 (over z, core), mdl: 4 (over y, x).
Axes of the slice: x: 2, y: 2, z: 4, core: 2. Of those that a mesh axis runs over, the one named last changes fastest.
Arguments:
- hidden_in: bfloat16 [8, 2228224], P('tok', 'mdl'), may hold values from -6 to 6
- doc_ids: int32 [16384], P('tok'), may hold values from 0 to 2, as said below
- ln1_gain: float32 [1088], replicated, may hold values from 0.25 to 1.75
- ln1_bias: float32 [1088], replicated, may hold values from -3 to 3
- w_qkv: bfloat16 [1088, 3264], P('tok', 'mdl'), may hold values from -0.25 to 0.25
- q_bias: float32 [1088], replicated, may hold values from -3 to 3
- v_bias: float32 [1088], replicated, may hold values from -3 to 3
- w_out: bfloat16 [1088, 1088], P('tok', 'mdl'), may hold values from -1 to 1
- out_bias: float32 [1088], replicated, may hold values from -3 to 3
- ln2_gain: float32 [1088], replicated, may hold values from 0.25 to 1.75
- ln2_bias: float32 [1088], replicated, may hold values from -3 to 3
- w_fc1: bfloat16 [1088, 4352], P('tok', 'mdl'), may hold values from -0.1875 to 0.1875
- fc1_bias: float32 [4352], replicated, may hold values from -3 to 3
- w_fc2: bfloat16 [4352, 1088], P('tok', 'mdl'), may hold values from -0.09375 to 0.09375
- fc2_bias: float32 [1088], replicated, may hold values from -3 to 3
- cotangent: bfloat16 [8, 2228224], P('tok', 'mdl'), may hold values from -6 to 6
Outputs:
- result: bfloat16 [8, 2228224], P('tok', 'mdl')
- input_grad: bfloat16 [8, 2228224], P('tok', 'mdl')
- w_qkv_grad: float32 [1088, 3264], P('tok', 'mdl')
- w_out_grad: float32 [1088, 1088], P('tok', 'mdl')
- w_fc1_grad: float32 [1088, 4352], P('tok', 'mdl')
- w_fc2_grad: float32 [4352, 1088], P('tok', 'mdl')
- ln1_gain_grad: float32 [1088], replicated
- ln1_bias_grad: float32 [1088], replicated
- q_bias_grad: float32 [1088], replicated
- v_bias_grad: float32 [1088], replicated
- out_bias_grad: float32 [1088], replicated
- ln2_gain_grad: float32 [1088], replicated
- ln2_bias_grad: float32 [1088], replicated
- fc1_bias_grad: float32 [4352], replicated
- fc2_bias_grad: float32 [1088], replicated
The draws below stay inside these ranges and needn't reach their ends.
Inputs may be any that keep to these rules, and one draw needn't show every extreme that they name: `doc_ids`: every window of 2048 tokens holds exactly three documents numbered 0, 1, 2 in token order; document 0 ends within the window's first 512 tokens and document 2 starts within its last 512 tokens.
All inputs are finite; a program needn't handle non-finite values.
Results may differ from the reference program's by a relative error of at most 0.017.
Values may be sent and summed in bfloat16 or wider, within the bound.
A program may use at most 448 MiB of HBM per device.

```python
import jax
import jax.numpy as jnp
from jax import lax

D = 1088
HEADS = 17
HEAD_DIM = 64
FF = 4352
SEQ = 2048
TOKENS = 16384
PIECE = 512


def draw_doc_ids(key, part):
    key = jax.random.fold_in(key, 7)
    first_key, last_key = jax.random.split(key)
    window_count = TOKENS // SEQ
    first_end = jax.random.randint(first_key, (window_count, 1), 1, PIECE)
    last_start = jax.random.randint(last_key, (window_count, 1), SEQ - PIECE + 1, SEQ)
    position = jnp.arange(SEQ)[None, :]
    numbers = (position >= first_end).astype(jnp.int32) + (position >= last_start).astype(jnp.int32)
    return numbers.reshape(TOKENS).astype(jnp.int32)


def steps_of(stream_key, dims, pieces, low, high):
    def one(dim, parts):
        heights = jax.random.uniform(jax.random.fold_in(jax.random.fold_in(stream_key, 6), dim), (parts,), jnp.float32, low / len(pieces), high / len(pieces))
        return jnp.repeat(jnp.exp(heights), dims[dim] // parts).reshape((-1,) + (1,) * (len(dims) - dim - 1))

    level = one(*pieces[0])
    for cut in pieces[1:]:
        level = level * one(*cut)
    return level


def normal_values(rng, extent, width, limit, cuts=(), held_as=jnp.bfloat16):
    level = steps_of(rng, extent, cuts, -0.22, 0.18) if cuts else 1.0
    entries = jax.random.normal(rng, extent, jnp.float32) * width * level
    return jnp.minimum(jnp.maximum(entries, -limit), limit).astype(held_as)


def setup_inputs(seed: int = 0) -> dict:
    key_of = jax.random.split(jax.random.key(seed), 17)
    hidden_in = normal_values(key_of[0], (TOKENS // SEQ, SEQ * D), 1.0, 6.0, ((0, 8), (1, 4)))
    doc_ids = draw_doc_ids(jax.random.fold_in(key_of[16], 71), 0)
    ln1_gain = jnp.clip(1.0 + 0.15 * jax.random.normal(key_of[2], (D,), jnp.float32), 0.25, 1.75)
    ln1_bias = normal_values(key_of[3], (D,), 0.5, 3.0, (), jnp.float32)
    w_qkv = normal_values(key_of[4], (D, 3 * D), (D // 2) ** -0.5, 0.25, ((0, 8), (1, 4)))
    q_bias = normal_values(key_of[5], (D,), 0.5, 3.0, (), jnp.float32)
    v_bias = normal_values(key_of[6], (D,), 0.5, 3.0, (), jnp.float32)
    w_out = normal_values(key_of[7], (D, D), (max(D // 32, 16)) ** -0.5, 1.0, ((0, 8), (1, 4)))
    out_bias = normal_values(key_of[8], (D,), 0.5, 3.0, (), jnp.float32)
    ln2_gain = jnp.clip(1.0 + 0.15 * jax.random.normal(key_of[9], (D,), jnp.float32), 0.25, 1.75)
    ln2_bias = normal_values(key_of[10], (D,), 0.5, 3.0, (), jnp.float32)
    w_fc1 = normal_values(key_of[11], (D, FF), D ** -0.5, 0.1875, ((0, 8), (1, 4)))
    fc1_bias = normal_values(key_of[12], (FF,), 0.5, 3.0, (), jnp.float32)
    w_fc2 = normal_values(key_of[13], (FF, D), FF ** -0.5, 0.09375, ((0, 8), (1, 4)))
    fc2_bias = normal_values(key_of[14], (D,), 0.5, 3.0, (), jnp.float32)
    cotangent = normal_values(key_of[15], (TOKENS // SEQ, SEQ * D), 1.0, 6.0, ((0, 8), (1, 4)))
    return {"hidden_in": hidden_in, "doc_ids": doc_ids, "ln1_gain": ln1_gain, "ln1_bias": ln1_bias, "w_qkv": w_qkv, "q_bias": q_bias, "v_bias": v_bias, "w_out": w_out, "out_bias": out_bias, "ln2_gain": ln2_gain, "ln2_bias": ln2_bias, "w_fc1": w_fc1, "fc1_bias": fc1_bias, "w_fc2": w_fc2, "fc2_bias": fc2_bias, "cotangent": cotangent}


EPSILON = 1e-05
SCORE_SCALE = 0.125
MASKED = -1e+30
HIGHEST = lax.Precision.HIGHEST

@jax.custom_vjp
def low(v):
    return lax.optimization_barrier(v.astype(jnp.bfloat16)).astype(jnp.float32)

@jax.custom_vjp
def low_back(v):
    return v

def low_keep(v):
    return (low(v), None)

def low_pass(kept, grad):
    return (grad,)

def back_keep(v):
    return (v, None)

def back_low(kept, grad):
    return (low(grad),)
low.defvjp(low_keep, low_pass)
low_back.defvjp(back_keep, back_low)

def normalize(values, gain_vec, shift_vec):
    centered = values - lax.optimization_barrier(jnp.mean(values, axis=-1, keepdims=True))
    scaled = centered * lax.rsqrt(lax.optimization_barrier(jnp.mean(centered * centered, axis=-1, keepdims=True)) + EPSILON)
    return scaled * gain_vec + shift_vec

def window_attention(window_items):
    query_block, key_block, value_block, doc_block = window_items
    position = jnp.arange(SEQ)
    raw_scores = jnp.einsum('qhd,khd->hqk', query_block, key_block, precision=HIGHEST) * SCORE_SCALE
    scores = low_back(raw_scores)
    visible = (doc_block[:, None] == doc_block[None, :]) & (position[None, :] <= position[:, None])
    scores = jnp.where(visible[None], scores, MASKED)
    top_score = lax.optimization_barrier(jnp.max(scores, axis=-1, keepdims=True))
    weights_raw = jnp.exp(scores - top_score)
    probs = weights_raw / lax.optimization_barrier(jnp.sum(weights_raw, axis=-1, keepdims=True))
    return jnp.einsum('hqk,khd->qhd', low(probs), value_block, precision=HIGHEST)

def reference(hidden_in, doc_ids, ln1_gain, ln1_bias, w_qkv, q_bias, v_bias, w_out, out_bias, ln2_gain, ln2_bias, w_fc1, fc1_bias, w_fc2, fc2_bias, cotangent):
    window_count = TOKENS // SEQ
    doc_windows = doc_ids.reshape(window_count, SEQ)

    def layer(inputs, gain_one, shift_one, qkv_weight, query_bias, value_bias, out_weight, out_shift, gain_two, shift_two, fc1_weight, fc1_shift, fc2_weight, fc2_shift):
        first_norm = low(normalize(inputs, gain_one, shift_one))
        middle_zero = jnp.zeros((D,), jnp.float32)
        qkv = low_back(jnp.dot(first_norm, qkv_weight, precision=HIGHEST)) + jnp.concatenate([query_bias, middle_zero, value_bias])
        queries = low(qkv[:, :D])
        key_rows = low(qkv[:, D:2 * D])
        value_rows = low(qkv[:, 2 * D:])

        def shaped(values):
            return values.reshape(window_count, SEQ, HEADS, HEAD_DIM)
        attended = lax.map(jax.checkpoint(window_attention), (shaped(queries), shaped(key_rows), shaped(value_rows), doc_windows))
        attended = low_back(low(attended.reshape(TOKENS, D)))
        middle = inputs + low_back(jnp.dot(attended, out_weight, precision=HIGHEST)) + out_shift
        second_norm = low(normalize(middle, gain_two, shift_two))
        pre = low_back(jnp.dot(second_norm, fc1_weight, precision=HIGHEST)) + fc1_shift
        activation = low(jax.nn.gelu(pre))
        return middle + low_back(jnp.dot(activation, fc2_weight, precision=HIGHEST)) + fc2_shift
    float_args = [hidden_in.reshape(TOKENS, D), ln1_gain, ln1_bias, w_qkv, q_bias, v_bias, w_out, out_bias, ln2_gain, ln2_bias, w_fc1, fc1_bias, w_fc2, fc2_bias]
    float_args = [value.astype(jnp.float32) for value in float_args]
    output, pullback = jax.vjp(layer, *float_args)
    grads = pullback(cotangent.reshape(TOKENS, D).astype(jnp.float32))
    result = output.astype(jnp.bfloat16).reshape(window_count, SEQ * D)
    input_grad = grads[0].astype(jnp.bfloat16).reshape(window_count, SEQ * D)
    return (result, input_grad, grads[3], grads[6], grads[10], grads[12], grads[1], grads[2], grads[4], grads[5], grads[7], grads[8], grads[9], grads[11], grads[13])
```

```python
import functools
import jax
import jax.numpy as jnp
from jax import lax
from jax.experimental import pallas as pl
from jax.experimental.pallas import tpu as pltpu
from jax.sharding import PartitionSpec as P

SEQ = 2048
HEAD_DIM = 64
SCORE_SCALE = 0.125
MASKED = -1e30
BLOCK = 256
EDGE = 512


def spans_of(block_index):
    start = block_index * BLOCK
    stop = start + BLOCK
    if start < EDGE or stop > SEQ - EDGE:
        spans = [(0, start, True, False), (start, stop, True, True)]
    else:
        spans = [(0, EDGE, True, False), (EDGE, start, False, False), (start, stop, False, True)]
    return [span for span in spans if span[1] > span[0]]


def dot_rows(left, right):
    return lax.dot_general(left, right, (((1,), (1,)), ((), ())), preferred_element_type=jnp.float32)


def dot_plain(left, right):
    return jnp.dot(left, right, preferred_element_type=jnp.float32)


def dot_cols(left, right):
    return lax.dot_general(left, right, (((0,), (0,)), ((), ())), preferred_element_type=jnp.float32)


def mask_scores(raw, span, doc_q, doc_row_ref):
    low, high, by_doc, causal = span
    keep = None
    if by_doc:
        keep = doc_q == doc_row_ref[0, :, low:high]
    if causal:
        row_pos = lax.broadcasted_iota(jnp.int32, raw.shape, 0)
        col_pos = lax.broadcasted_iota(jnp.int32, raw.shape, 1)
        below = col_pos <= row_pos
        keep = below if keep is None else keep & below
    return raw if keep is None else jnp.where(keep, raw, MASKED)


def attend_kernel(heads, q_ref, k_ref, v_ref, doc_col_ref, doc_row_ref, o_ref, lse_ref, qs, ks, vs, os):
    head = pl.program_id(1)
    for index in range(heads):
        @pl.when(head == index)
        def _():
            cols = slice(index * HEAD_DIM, (index + 1) * HEAD_DIM)
            qs[...] = q_ref[0, :, cols] * jnp.bfloat16(SCORE_SCALE)
            ks[...] = k_ref[0, :, cols]
            vs[...] = v_ref[0, :, cols]

    for block_index in range(SEQ // BLOCK):
        rows = slice(block_index * BLOCK, (block_index + 1) * BLOCK)
        query = qs[rows, :]
        doc_q = doc_col_ref[0, rows, :]
        spans = spans_of(block_index)
        scores = [
            mask_scores(dot_rows(query, ks[span[0] : span[1], :]), span, doc_q, doc_row_ref)
            for span in spans
        ]
        top = functools.reduce(
            jnp.maximum, [jnp.max(part, axis=-1, keepdims=True) for part in scores]
        )
        parts = [jnp.exp(part - top) for part in scores]
        total = sum(jnp.sum(part, axis=-1, keepdims=True) for part in parts)
        mixed = sum(
            dot_plain(part.astype(jnp.bfloat16), vs[span[0] : span[1], :])
            for part, span in zip(parts, spans)
        )
        os[rows, :] = (mixed / total).astype(jnp.bfloat16)
        lse_ref[0, rows, :] = top + jnp.log(total)
    for index in range(heads):
        @pl.when(head == index)
        def _():
            o_ref[0, :, index * HEAD_DIM : (index + 1) * HEAD_DIM] = os[...]


def attend_back_kernel(
    heads, q_ref, k_ref, v_ref, o_ref, do_ref, lse_ref, doc_col_ref, doc_row_ref,
    dq_ref, dk_ref, dv_ref, qs, ks, vs, os, dos, dqs, dks, dvs,
):
    head = pl.program_id(1)
    for index in range(heads):
        @pl.when(head == index)
        def _():
            cols = slice(index * HEAD_DIM, (index + 1) * HEAD_DIM)
            qs[...] = q_ref[0, :, cols] * jnp.bfloat16(SCORE_SCALE)
            ks[...] = k_ref[0, :, cols]
            vs[...] = v_ref[0, :, cols]
            os[...] = o_ref[0, :, cols]
            dos[...] = do_ref[0, :, cols]

    for block_index in reversed(range(SEQ // BLOCK)):
        rows = slice(block_index * BLOCK, (block_index + 1) * BLOCK)
        query = qs[rows, :]
        grad = dos[rows, :]
        doc_q = doc_col_ref[0, rows, :]
        total = lse_ref[0, rows, :]
        centre = jnp.sum(
            grad.astype(jnp.float32) * os[rows, :].astype(jnp.float32), axis=-1, keepdims=True
        )
        d_query = None
        for span in spans_of(block_index):
            keys = slice(span[0], span[1])
            scores = mask_scores(dot_rows(query, ks[keys, :]), span, doc_q, doc_row_ref)
            probs = jnp.exp(scores - total)
            d_probs = dot_rows(grad, vs[keys, :])
            d_scores = (probs * (d_probs - centre)).astype(jnp.bfloat16)
            d_value = dot_cols(probs.astype(jnp.bfloat16), grad)
            d_key = dot_cols(d_scores, query)
            part = dot_plain(d_scores, ks[keys, :])
            d_query = part if d_query is None else d_query + part
            if block_index == SEQ // BLOCK - 1:
                dvs[keys, :] = d_value
                dks[keys, :] = d_key
            else:
                dvs[keys, :] += d_value
                dks[keys, :] += d_key
        dqs[rows, :] = (d_query * SCORE_SCALE).astype(jnp.bfloat16)
    for index in range(heads):
        @pl.when(head == index)
        def _():
            cols = slice(index * HEAD_DIM, (index + 1) * HEAD_DIM)
            dq_ref[0, :, cols] = dqs[...]
            dk_ref[0, :, cols] = dks[...].astype(jnp.bfloat16)
            dv_ref[0, :, cols] = dvs[...].astype(jnp.bfloat16)


VMEM_LIMIT = 48 * 1024 * 1024


def attention_forward(queries, keys, values, doc_col, doc_row):
    windows, _, width = queries.shape
    heads = width // HEAD_DIM
    whole = pl.BlockSpec((1, SEQ, width), lambda w, h: (w, 0, 0))
    stat = pl.BlockSpec((1, SEQ, 1), lambda w, h: (w * heads + h, 0, 0))
    return pl.pallas_call(
        functools.partial(attend_kernel, heads),
        grid=(windows, heads),
        in_specs=[
            whole, whole, whole,
            pl.BlockSpec((1, SEQ, 1), lambda w, h: (w, 0, 0)),
            pl.BlockSpec((1, 1, SEQ), lambda w, h: (w, 0, 0)),
        ],
        out_specs=[whole, stat],
        out_shape=[
            jax.ShapeDtypeStruct(queries.shape, jnp.bfloat16),
            jax.ShapeDtypeStruct((windows * heads, SEQ, 1), jnp.float32),
        ],
        scratch_shapes=[pltpu.VMEM((SEQ, HEAD_DIM), jnp.bfloat16)] * 4,
        compiler_params=pltpu.CompilerParams(vmem_limit_bytes=VMEM_LIMIT),
        cost_estimate=pl.CostEstimate(
            flops=windows * heads * SEQ * SEQ * HEAD_DIM * 8,
            bytes_accessed=windows * SEQ * width * 8,
            transcendentals=windows * heads * SEQ * SEQ // 2,
        ),
    )(queries, keys, values, doc_col, doc_row)


def attention_backward(queries, keys, values, mixed, grads, lse, doc_col, doc_row):
    windows, _, width = queries.shape
    heads = width // HEAD_DIM
    whole = pl.BlockSpec((1, SEQ, width), lambda w, h: (w, 0, 0))
    stat = pl.BlockSpec((1, SEQ, 1), lambda w, h: (w * heads + h, 0, 0))
    return pl.pallas_call(
        functools.partial(attend_back_kernel, heads),
        grid=(windows, heads),
        in_specs=[
            whole, whole, whole, whole, whole, stat,
            pl.BlockSpec((1, SEQ, 1), lambda w, h: (w, 0, 0)),
            pl.BlockSpec((1, 1, SEQ), lambda w, h: (w, 0, 0)),
        ],
        out_specs=[whole, whole, whole],
        out_shape=[jax.ShapeDtypeStruct(queries.shape, jnp.bfloat16)] * 3,
        scratch_shapes=[pltpu.VMEM((SEQ, HEAD_DIM), jnp.bfloat16)] * 6
        + [pltpu.VMEM((SEQ, HEAD_DIM), jnp.float32)] * 2,
        compiler_params=pltpu.CompilerParams(vmem_limit_bytes=VMEM_LIMIT),
        cost_estimate=pl.CostEstimate(
            flops=windows * heads * SEQ * SEQ * HEAD_DIM * 20,
            bytes_accessed=windows * SEQ * width * 16,
            transcendentals=windows * heads * SEQ * SEQ // 2,
        ),
    )(queries, keys, values, mixed, grads, lse, doc_col, doc_row)


D = 1088
HEADS = 17
EPSILON = 1e-05
GELU_A = 0.7978845608028654
GELU_B = 0.044715


def normalize(values, gain_vec, shift_vec):
    centered = values - jnp.mean(values, axis=-1, keepdims=True)
    inv_root = lax.rsqrt(jnp.mean(centered * centered, axis=-1, keepdims=True) + EPSILON)
    scaled = centered * inv_root
    return (scaled * gain_vec + shift_vec, scaled, inv_root)


def normalize_back(gradient, scaled, inv_root, gain_vec):
    weighted = gradient * gain_vec
    inner = (
        weighted
        - jnp.mean(weighted, axis=-1, keepdims=True)
        - scaled * jnp.mean(weighted * scaled, axis=-1, keepdims=True)
    )
    return (inv_root * inner, jnp.sum(gradient * scaled, axis=0), jnp.sum(gradient, axis=0))


def gather_weight(weight):
    rows = lax.all_gather(weight, "tok", axis=0, tiled=True)
    return lax.all_gather(rows, "mdl", axis=1, tiled=True)


def scatter_grad(grad):
    rows = lax.psum_scatter(grad.astype(jnp.bfloat16), "tok", scatter_dimension=0, tiled=True)
    return lax.psum_scatter(rows, "mdl", scatter_dimension=1, tiled=True).astype(jnp.float32)


def body(
    hidden_in, doc_ids, ln1_gain, ln1_bias, w_qkv, q_bias, v_bias, w_out, out_bias,
    ln2_gain, ln2_bias, w_fc1, fc1_bias, w_fc2, fc2_bias, cotangent,
):
    groups = lax.axis_size("mdl")
    windows = hidden_in.shape[0]
    piece_len = hidden_in.shape[1] // D
    row_total = windows * piece_len
    width = -(-HEADS // groups) * HEAD_DIM
    x = hidden_in.reshape(row_total, D).astype(jnp.float32)
    cot_low = cotangent.reshape(row_total, D)
    cot = cot_low.astype(jnp.float32)
    qkv_full = gather_weight(w_qkv)
    out_full = gather_weight(w_out)
    fc1_full = gather_weight(w_fc1)
    fc2_full = gather_weight(w_fc2)

    def to_heads(rows):
        padded = jnp.pad(rows, ((0, 0), (0, groups * width - D)))
        parts = padded.reshape(windows, piece_len, groups, width)
        swapped = lax.all_to_all(parts, "mdl", split_axis=2, concat_axis=1, tiled=True)
        return swapped.reshape(windows, groups * piece_len, width)

    def to_rows(parts):
        split = parts.reshape(windows, groups, piece_len, width)
        swapped = lax.all_to_all(split, "mdl", split_axis=1, concat_axis=3, tiled=True)
        return swapped.reshape(row_total, groups * width)[:, :D]

    doc_row = doc_ids.reshape(windows, 1, SEQ)
    doc_col = doc_ids.reshape(windows, SEQ, 1)

    first, scaled_one, inv_one = normalize(x, ln1_gain, ln1_bias)
    h1 = first.astype(jnp.bfloat16)
    q_rows = (dot_plain(h1, qkv_full[:, :D]) + q_bias).astype(jnp.bfloat16)
    k_rows = dot_plain(h1, qkv_full[:, D : 2 * D]).astype(jnp.bfloat16)
    v_rows = (dot_plain(h1, qkv_full[:, 2 * D :]) + v_bias).astype(jnp.bfloat16)
    q_heads, k_heads, v_heads = to_heads(q_rows), to_heads(k_rows), to_heads(v_rows)
    mixed, lse = attention_forward(q_heads, k_heads, v_heads, doc_col, doc_row)
    attn = to_rows(mixed)
    mid = x + dot_plain(attn, out_full) + out_bias
    second, scaled_two, inv_two = normalize(mid, ln2_gain, ln2_bias)
    h2 = second.astype(jnp.bfloat16)
    pre = dot_plain(h2, fc1_full) + fc1_bias
    tanh = jnp.tanh(GELU_A * (pre + GELU_B * pre * pre * pre))
    act = (0.5 * pre * (1.0 + tanh)).astype(jnp.bfloat16)
    slope = 0.5 * (1.0 + tanh) + 0.5 * pre * (1.0 - tanh * tanh) * GELU_A * (
        1.0 + 3.0 * GELU_B * pre * pre
    )
    result = mid + dot_plain(act, fc2_full) + fc2_bias

    grad_fc2 = scatter_grad(dot_cols(act, cot_low))
    d_pre = dot_rows(cot_low, fc2_full) * slope
    d_pre_low = d_pre.astype(jnp.bfloat16)
    grad_fc1 = scatter_grad(dot_cols(h2, d_pre_low))
    d_h2 = dot_rows(d_pre_low, fc1_full)
    d_norm, ln2_gain_grad, ln2_bias_grad = normalize_back(d_h2, scaled_two, inv_two, ln2_gain)
    d_mid = cot + d_norm
    d_mid_low = d_mid.astype(jnp.bfloat16)
    grad_out = scatter_grad(dot_cols(attn, d_mid_low))
    d_attn = dot_rows(d_mid_low, out_full).astype(jnp.bfloat16)
    dq, dk, dv = attention_backward(
        q_heads, k_heads, v_heads, mixed, to_heads(d_attn), lse, doc_col, doc_row
    )
    dq_rows, dk_rows, dv_rows = to_rows(dq), to_rows(dk), to_rows(dv)
    d_qkv = jnp.concatenate([dq_rows, dk_rows, dv_rows], axis=-1)
    grad_qkv = scatter_grad(dot_cols(h1, d_qkv))
    d_h1 = dot_rows(d_qkv, qkv_full)
    d_norm, ln1_gain_grad, ln1_bias_grad = normalize_back(d_h1, scaled_one, inv_one, ln1_gain)
    d_input = d_mid + d_norm
    sums = (
        ln1_gain_grad,
        ln1_bias_grad,
        jnp.sum(dq_rows.astype(jnp.float32), axis=0),
        jnp.sum(dv_rows.astype(jnp.float32), axis=0),
        jnp.sum(d_mid, axis=0),
        ln2_gain_grad,
        ln2_bias_grad,
        jnp.sum(d_pre, axis=0),
        jnp.sum(cot, axis=0),
    )
    flat = lax.psum(jnp.concatenate(sums), ("tok", "mdl"))
    cuts, place = [], 0
    for part in sums:
        cuts.append(flat[place : place + part.shape[0]])
        place += part.shape[0]
    return (
        result.astype(jnp.bfloat16).reshape(windows, piece_len * D),
        d_input.astype(jnp.bfloat16).reshape(windows, piece_len * D),
        grad_qkv,
        grad_out,
        grad_fc1,
        grad_fc2,
        *cuts,
    )


def solution(mesh):
    both, tok, none = P("tok", "mdl"), P("tok"), P()
    in_specs = (
        both, tok, none, none, both, none, none, both, none,
        none, none, both, none, both, none, both,
    )
    out_specs = (both,) * 6 + (none,) * 9
    return jax.shard_map(body, mesh=mesh, in_specs=in_specs, out_specs=out_specs, check_vma=False)
```
